512 devices in a mesh: span: 8 (over x, y_hi), seq: 64 (over y_lo, z, core).
Axes of the slice: x: 4, y: 8 (y_hi: 2, y_lo: 4; y = y_hi * 4 + y_lo), z: 8, core: 2. Of those that a mesh axis runs over, the one named last changes fastest.
Arguments:
- queries: bfloat16 [8, 1536, 4096], P('span', 'seq'), may hold values from -98 to 98
- key_rows: bfloat16 [8, 1536, 4096], P('span', 'seq'), may hold values from -4.1 to 4.1
- value_rows: bfloat16 [8, 1536, 4096], P('span', 'seq'), may hold values from -6 to 6
- block_mask: int32 [8, 8], replicated, may hold values from 0 to 1, as said below
- noise_level: int32 [8], replicated, may hold values from 0 to 7
- gate_table: float32 [8, 4096], replicated, may hold values from 2 to 16
Outputs:
- attended: bfloat16 [8, 1536, 4096], P('span', 'seq')
The draws below stay inside these ranges and needn't reach their ends.
Inputs may be any that keep to these rules, and one draw needn't show every extreme that they name: block_mask[c][c] is 1 for every block c; block_mask[c][c2] is 0 where c2 > c or c2 < c - 2.
All inputs are finite; a program needn't handle non-finite values.
Results may differ from the reference program's by a relative error of at most 0.0065.
Values may be sent and summed in bfloat16 or wider, within the bound.
No kernel may reach another device: no remote copies, remote signals or barrier semaphores. Data moves between devices by JAX's collectives and lax.ppermute only.
A program may use at most 64 MiB of HBM per device.

```python
import math
import jax
import jax.numpy as jnp
from jax import lax

HD = 128
HEADS = 32
WINDOW = 2
LEVELS = 8
FEATURES = 4096
SPANS = 8
SEQ_LEN = 1536


def pair_keys(key):
    key_field = jnp.clip(jax.random.normal(key, (SPANS, SEQ_LEN, FEATURES), jnp.float32), -4.0, 4.0)
    row_index = jnp.arange(SEQ_LEN)
    echoed = (row_index % 61 == 1)[None, :, None]
    return jnp.where(echoed, key_field, key_field)


def draw_key_rows(key, part):
    key_field = pair_keys(key)
    return key_field.astype(jnp.bfloat16)


def draw_queries(key, part):
    key = jax.random.fold_in(key, 7)
    result = jnp.clip(2.0 * jax.random.normal(key, (SPANS, SEQ_LEN, FEATURES), jnp.float32), -12.0, 12.0)
    return result.astype(jnp.bfloat16)


def draw_block_mask(key, part):
    key = jax.random.fold_in(key, 5)
    coins = jax.random.randint(key, (SPANS, SPANS), 0, 4)
    target = jnp.arange(SPANS)[:, None]
    source_col = jnp.arange(SPANS)[None, :]
    inside = jnp.logical_and(source_col < target, source_col >= target - WINDOW)
    picked = jnp.where(jnp.logical_and(inside, coins > 0), 1, 0)
    return jnp.where(source_col == target, 1, picked).astype(jnp.int32)


def with_ends(values, own_key, least, top_value):
    longest = values.shape.index(max(values.shape))
    spots = []
    for shift in (0, 1):
        where = [jax.random.randint(jax.random.fold_in(own_key, axis), (), 0, length) for axis, length in enumerate(values.shape)]
        where[longest] = (where[longest] + shift) % values.shape[longest]
        spots.append(tuple(where))
    return values.at[spots[0]].set(least).at[spots[1]].set(top_value)


def block_levels(stream_key, extent, cuts, smallest, largest):
    def one(axis_at, parts):
        steps = jax.random.uniform(jax.random.fold_in(jax.random.fold_in(stream_key, 6), axis_at), (parts,), jnp.float32, smallest / len(cuts), largest / len(cuts))
        return jnp.repeat(jnp.exp(steps), extent[axis_at] // parts).reshape((-1,) + (1,) * (len(extent) - axis_at - 1))

    gain = one(*cuts[0])
    for cut in cuts[1:]:
        gain = gain * one(*cut)
    return gain


def normal_values(rng, dims, scale, bound, shards=(), kind=jnp.bfloat16):
    entries = jax.random.normal(rng, dims, jnp.float32) * scale
    if len(shards) > 0:
        entries = block_levels(rng, dims, shards, -0.22, 0.18) * entries
    return jnp.clip(entries, min=-bound, max=bound).astype(kind)


def setup_inputs(seed: int = 0) -> dict:
    key_list = jax.random.split(jax.random.key(seed), 7)
    queries = draw_queries(jax.random.fold_in(key_list[6], 71), 0)
    key_rows = draw_key_rows(jax.random.fold_in(key_list[6], 71), 0)
    value_rows = normal_values(key_list[2], (SPANS, SEQ_LEN, FEATURES), 1.0, 6.0, ((0, 8), (1, 64)))
    block_mask = draw_block_mask(jax.random.fold_in(key_list[6], 71), 0)
    noise_level = with_ends(jax.random.randint(key_list[4], (SPANS,), 0, LEVELS), jax.random.fold_in(key_list[4], 1), 0, LEVELS - 1).astype(jnp.int32)
    gate_table = jnp.clip(jnp.exp(jax.random.uniform(key_list[5], (LEVELS, FEATURES), jnp.float32, math.log(2.0), math.log(16.0))), 2.0, 16.0)
    return {"queries": queries, "key_rows": key_rows, "value_rows": value_rows, "block_mask": block_mask, "noise_level": noise_level, "gate_table": gate_table}


def reference(queries, key_rows, value_rows, block_mask, noise_level, gate_table):
    scaling = HD ** -0.5

    def one_span(span_at):
        key_parts = []
        value_parts = []
        flags = []
        for distance in range(WINDOW + 1):
            source = jnp.maximum(span_at - distance, 0).astype(jnp.int32)
            key_parts.append(lax.dynamic_index_in_dim(key_rows, source, 0, keepdims=False))
            value_parts.append(lax.dynamic_index_in_dim(value_rows, source, 0, keepdims=False))
            usable = jnp.logical_and(span_at - distance >= 0, block_mask[span_at, source] > 0)
            flags.append(jnp.broadcast_to(usable, (SEQ_LEN,)))
        key_window = jnp.concatenate(key_parts, axis=0)
        value_window = jnp.concatenate(value_parts, axis=0)
        usable_keys = jnp.concatenate(flags, axis=0)
        query_block = lax.dynamic_index_in_dim(queries, span_at, 0, keepdims=False)
        gate_row = lax.dynamic_index_in_dim(gate_table, noise_level[span_at], 0, keepdims=False)

        def one_head(head_at):
            start = head_at * HD
            query_head = lax.dynamic_slice_in_dim(query_block, start, HD, 1)
            key_head = lax.dynamic_slice_in_dim(key_window, start, HD, 1)
            value_head = lax.dynamic_slice_in_dim(value_window, start, HD, 1)
            scores = jnp.dot(query_head, key_head.T, preferred_element_type=jnp.float32) * scaling
            maxima = jnp.max(jnp.where(usable_keys[None, :], scores, -jnp.inf), axis=1, keepdims=True)
            expos = jnp.where(usable_keys[None, :], jnp.exp(scores - maxima), 0.0)
            numerator = jnp.dot(expos.astype(jnp.bfloat16), value_head, preferred_element_type=jnp.float32)
            heard = numerator / jnp.sum(expos, axis=1, keepdims=True)
            gate_part = lax.dynamic_slice_in_dim(gate_row, start, HD, 0)
            return (heard * gate_part[None, :]).astype(jnp.bfloat16)

        per_head = lax.map(one_head, jnp.arange(HEADS, dtype=jnp.int32))
        return per_head.transpose(1, 0, 2).reshape(SEQ_LEN, FEATURES)

    return lax.map(one_span, jnp.arange(SPANS, dtype=jnp.int32))
```

```python
import functools

import jax
import jax.numpy as jnp
from jax import lax
from jax.experimental import pallas as pl
from jax.experimental.pallas import tpu as pltpu
from jax.sharding import PartitionSpec as P

HD = 128
WINDOW = 2
LOG2E = 1.4426950408889634
VMEM_LIMIT = 48 * 1024 * 1024


def attend(first, last, scale, flag_ref, q_ref, kv_ref, kvx_ref, *rest):
    if first:
        state_in = None
    else:
        state_in, rest = rest[:3], rest[3:]
    if last:
        gate_ref, out_ref = rest
    else:
        m_out, l_out, a_out = rest
    rows = q_ref.shape[0]
    tile = min(256, rows)
    const = scale * LOG2E

    def whole(t, with_keys):
        at = pl.ds(t * tile, tile)
        if with_keys:
            q = q_ref[at, :]
            dims = (((1,), (1,)), ((), ()))
            scores = [
                lax.dot_general(q, ref[0], dims, preferred_element_type=jnp.float32)
                for ref in (kv_ref, kvx_ref)
            ]
            top = jnp.maximum(scores[0].max(axis=1, keepdims=True), scores[1].max(axis=1, keepdims=True))
            if not first:
                before = state_in[0][at, :1]
                top = jnp.maximum(top, before)
            expos = [jnp.exp2((s - top) * const) for s in scores]
            total = expos[0].sum(axis=1, keepdims=True) + expos[1].sum(axis=1, keepdims=True)
            heard = sum(
                jnp.dot(e.astype(jnp.bfloat16), ref[1], preferred_element_type=jnp.float32)
                for e, ref in zip(expos, (kv_ref, kvx_ref))
            )
            if not first:
                shrink = jnp.exp2((before - top) * const)
                total = total + state_in[1][at, :1] * shrink
                heard = heard + state_in[2][at, :] * shrink
        else:
            top, total, heard = state_in[0][at, :1], state_in[1][at, :1], state_in[2][at, :]
        if last:
            out_ref[at, :] = (heard / total * gate_ref[...]).astype(jnp.bfloat16)
        else:
            m_out[at, :] = jnp.broadcast_to(top, (tile, HD))
            l_out[at, :] = jnp.broadcast_to(total, (tile, HD))
            a_out[at, :] = heard

    def run(with_keys):
        for t in range(rows // tile):
            whole(t, with_keys)

    if first:
        run(True)
    else:
        usable = flag_ref[0] > 0

        @pl.when(usable)
        def _():
            run(True)

        @pl.when(jnp.logical_not(usable))
        def _():
            run(False)


def step(flag, q, kv, kvx, state=None, gate=None):
    first, last = state is None, gate is not None
    rows, keys = q.shape[0], 2 * kv.shape[1]
    vmem = pl.BlockSpec(memory_space=pltpu.VMEM)
    operands = [flag, q, kv, kvx] + list(state or ()) + ([gate] if last else [])
    in_specs = [pl.BlockSpec(memory_space=pltpu.SMEM)] + [vmem] * (len(operands) - 1)
    stat = jax.ShapeDtypeStruct((rows, HD), jnp.float32)
    out_shape = jax.ShapeDtypeStruct((rows, HD), jnp.bfloat16) if last else (stat, stat, stat)
    return pl.pallas_call(
        functools.partial(attend, first, last, HD ** -0.5),
        out_shape=out_shape,
        in_specs=in_specs,
        out_specs=vmem if last else (vmem,) * 3,
        compiler_params=pltpu.CompilerParams(vmem_limit_bytes=VMEM_LIMIT),
        cost_estimate=pl.CostEstimate(
            flops=4 * rows * keys * HD, bytes_accessed=4 * rows * HD * 8, transcendentals=rows * keys
        ),
    )(*operands)


def on_device(queries, key_rows, value_rows, block_mask, noise_level, gate_table):
    local = queries.shape[1]
    heads = queries.shape[2] // HD
    group = lax.axis_size("seq")
    spans = lax.axis_size("span")
    cores = group // heads
    chips = [[h * cores + c for h in range(heads)] for c in range(cores)]
    rows = heads * local
    position = lax.axis_index("seq")
    span_at = lax.axis_index("span")
    head = position // cores

    def exchange(block):
        return lax.all_to_all(
            block, "seq", split_axis=0, concat_axis=0, axis_index_groups=chips, tiled=True
        )

    def from_earlier(block, distance):
        return lax.ppermute(block, "span", [(i, i + distance) for i in range(spans - distance)])

    def other_core(block):
        return lax.ppermute(block, "seq", [(i, i ^ 1) for i in range(group)])

    def allowed(distance):
        column = span_at - distance
        usable = jnp.logical_and(column >= 0, block_mask[span_at, jnp.maximum(column, 0)] > 0)
        return usable.astype(jnp.int32).reshape(1)

    mixed = jnp.concatenate((queries[0], key_rows[0], value_rows[0]), axis=0)
    mixed = mixed.reshape(3 * local, heads, HD).transpose(1, 0, 2)
    got = exchange(mixed)
    q = got[:, :local].reshape(rows, HD)
    kv = got[:, local:].reshape(heads, 2, local, HD).transpose(1, 0, 2, 3).reshape(2, rows, HD)

    kv1 = from_earlier(kv, 1)
    kv2 = from_earlier(kv, 2)
    kvx = other_core(kv)
    state = step(allowed(0), q, kv, kvx)
    kv2x = other_core(kv2)
    state = step(allowed(2), q, kv2, kv2x, state)
    kv1x = other_core(kv1)
    gate_row = lax.dynamic_slice(
        gate_table, (noise_level[span_at], head * HD), (1, HD)
    )
    out = step(allowed(1), q, kv1, kv1x, state, gate_row)

    back = exchange(out.reshape(heads, local, HD))
    return back.transpose(1, 0, 2).reshape(1, local, heads * HD)


def solution(mesh):
    in_specs = (
        P("span", "seq", None),
        P("span", "seq", None),
        P("span", "seq", None),
        P(),
        P(),
        P(),
    )
    out_specs = P("span", "seq", None)
    return jax.shard_map(
        on_device, mesh=mesh, in_specs=in_specs, out_specs=out_specs, check_vma=False
    )
```

```python
import functools

import jax
import jax.numpy as jnp
from jax import lax
from jax.experimental import pallas as pl
from jax.experimental.pallas import tpu as pltpu
from jax.sharding import Mesh
from jax.sharding import PartitionSpec as P

HD = 128
SPAN = ("x", "y_hi")
CHIPS = ("y_lo", "z")
CONST = HD ** (-0.5) * 1.4426950408889634
TILE = 384
VMEM_LIMIT = 48 * 1024 * 1024


def weigh(q, halves, top, const):
    dims = (((1,), (1,)), ((), ()))
    scores = [lax.dot_general(q, ref[0], dims, preferred_element_type=jnp.float32) for ref in halves]
    own = jnp.maximum(scores[0].max(axis=1, keepdims=True), scores[1].max(axis=1, keepdims=True))
    top, less = top(own)
    expos = [jnp.exp2((s - less) * const) for s in scores]
    total = expos[0].sum(axis=1, keepdims=True) + expos[1].sum(axis=1, keepdims=True)
    heard = sum(
        jnp.dot(e.astype(jnp.bfloat16), ref[1], preferred_element_type=jnp.float32)
        for e, ref in zip(expos, halves)
    )
    return top, total, heard


def diagonal():
    return lax.broadcasted_iota(jnp.int32, (HD, HD), 0) == lax.broadcasted_iota(jnp.int32, (HD, HD), 1)


def own_block(mask_ref, level_ref, gate_ref, q_ref, kv_ref, m_out, l_out, a_out, aux_out):
    span_at = lax.axis_index(SPAN)
    for distance in (1, 2):
        column = span_at - distance
        usable = jnp.logical_and(column >= 0, mask_ref[span_at, jnp.maximum(column, 0)] > 0)
        value = jnp.where(usable, 1.0, 0.0).astype(jnp.float32)
        aux_out[pl.ds((distance - 1) * 8, 8), :] = jnp.full((8, HD), value, jnp.float32)
    head = lax.axis_index(CHIPS)
    mine = gate_ref[:, pl.ds(pl.multiple_of(head * HD, HD), HD)]
    chosen = lax.broadcasted_iota(jnp.int32, mine.shape, 0) == level_ref[span_at]
    gate = jnp.where(chosen, mine, 0.0).sum(axis=0, keepdims=True)
    aux_out[pl.ds(16, 8), :] = jnp.broadcast_to(gate, (8, HD))
    for t in range(q_ref.shape[0] // TILE):
        at = pl.ds(t * TILE, TILE)
        top, total, heard = weigh(q_ref[at, :], (kv_ref.at[0], kv_ref.at[1]), lambda own: (own, own), CONST)
        m_out[at, :] = jnp.broadcast_to(top, (TILE, HD))
        l_out[at, :] = jnp.broadcast_to(total, (TILE, HD))
        a_out[at, :] = heard


def served_block(q_ref, kv_ref, out_ref):
    rows = q_ref.shape[0]
    eye = diagonal()
    stats = []
    for t in range(rows // TILE):
        at = pl.ds(t * TILE, TILE)
        top, total, heard = weigh(q_ref[at, :], (kv_ref.at[0], kv_ref.at[1]), lambda own: (own, own), CONST)
        out_ref[at, :] = (heard / total).astype(jnp.bfloat16)
        level = top + jnp.log2(total) * (1.0 / CONST)
        for j in range(TILE // HD):
            stats.append(jnp.where(eye, level[j * HD : (j + 1) * HD], 0.0).sum(axis=0, keepdims=True))
    spare = 8 - len(stats)
    level = jnp.concatenate(stats + [jnp.zeros((spare, HD), jnp.float32)], axis=0)
    high = level.astype(jnp.bfloat16).astype(jnp.float32)
    middle = (level - high).astype(jnp.bfloat16).astype(jnp.float32)
    low = level - high - middle
    pieces = jnp.concatenate((high, middle, low, jnp.zeros((8, HD), jnp.float32)), axis=0)
    out_ref[pl.ds(rows, 32), :] = pieces.astype(jnp.bfloat16)


def last_block(aux_ref, q_ref, kv_ref, m_in, l_in, a_in, part_ref, out_ref):
    rows = q_ref.shape[0]
    opened1 = aux_ref[0:1, :1] > 0.5
    opened2 = aux_ref[8:9, :1] > 0.5
    gate = aux_ref[16:17, :]
    eye = diagonal()
    pieces = part_ref[pl.ds(rows, 32), :].astype(jnp.float32)
    level = pieces[0:8] + pieces[8:16] + pieces[16:24]
    for t in range(rows // TILE):
        at = pl.ds(t * TILE, TILE)
        before = m_in[at, :1]
        served = jnp.concatenate(
            [
                jnp.where(eye, level[j : j + 1], 0.0).sum(axis=1, keepdims=True)
                for j in range(t * TILE // HD, (t + 1) * TILE // HD)
            ],
            axis=0,
        )
        known = jnp.where(opened2, jnp.maximum(before, served), before)

        def joined(own):
            top = jnp.where(opened1, jnp.maximum(own, known), known)
            return top, jnp.where(opened1, top, 1e30)

        top, total, heard = weigh(q_ref[at, :], (kv_ref.at[0], kv_ref.at[1]), joined, CONST)
        shrink = jnp.exp2((before - top) * CONST)
        share = jnp.where(opened2, jnp.exp2((jnp.where(opened2, served, top) - top) * CONST), 0.0)
        total = total + l_in[at, :1] * shrink + share
        heard = heard + a_in[at, :] * shrink + part_ref[at, :].astype(jnp.float32) * share
        out_ref[at, :] = (heard / total * gate).astype(jnp.bfloat16)


def call(kernel, out_shape, scalars, *arrays):
    vmem = pl.BlockSpec(memory_space=pltpu.VMEM)
    smem = pl.BlockSpec(memory_space=pltpu.SMEM)
    return pl.pallas_call(
        kernel,
        out_shape=out_shape,
        in_specs=[smem] * len(scalars) + [vmem] * len(arrays),
        out_specs=[vmem] * len(out_shape),
        compiler_params=pltpu.CompilerParams(vmem_limit_bytes=VMEM_LIMIT),
        cost_estimate=pl.CostEstimate(flops=1024, bytes_accessed=1024, transcendentals=0),
    )(*scalars, *arrays)


def on_device(queries, key_rows, value_rows, block_mask, noise_level, gate_table):
    local = queries.shape[1]
    heads = queries.shape[2] // HD
    spans = lax.axis_size(SPAN)
    rows = heads * local

    def exchange(block):
        return lax.all_to_all(block, CHIPS, split_axis=0, concat_axis=0, tiled=True)

    def moved(block, distance):
        route = [(i, i + distance) for i in range(spans) if 0 <= i + distance < spans]
        return lax.ppermute(block, SPAN, route)

    def other_core(block):
        return lax.ppermute(block, "core", [(0, 1), (1, 0)])

    def both_cores(block):
        return lax.all_gather(block, "core")

    mixed = jnp.concatenate((queries[0], key_rows[0], value_rows[0]), axis=0)
    mixed = mixed.reshape(3 * local, heads, HD).transpose(1, 0, 2)
    got = exchange(mixed)
    q = got[:, :local].reshape(rows, HD)
    kv = got[:, local:].reshape(heads, 2, local, HD).transpose(1, 0, 2, 3).reshape(2, rows, HD)

    stat = jax.ShapeDtypeStruct((rows, HD), jnp.float32)
    aux = jax.ShapeDtypeStruct((24, HD), jnp.float32)
    part = jax.ShapeDtypeStruct((rows + 32, HD), jnp.bfloat16)
    kv1 = moved(kv, 1)
    later_q = moved(q, -2)
    kv0 = both_cores(kv)
    *state, aux = call(own_block, [stat, stat, stat, aux], (block_mask, noise_level), gate_table, q, kv0)
    later_q, *state = lax.optimization_barrier((later_q, *state))
    (served,) = call(served_block, [part], (), later_q, kv0)
    part2 = moved(served, 2)
    kv1 = both_cores(kv1)
    (out,) = call(
        last_block, [jax.ShapeDtypeStruct((rows, HD), jnp.bfloat16)], (), aux, q, kv1, *state, part2
    )

    back = exchange(out.reshape(heads, local, HD))
    return back.transpose(1, 0, 2).reshape(1, local, heads * HD)


def solution(mesh):
    parts = Mesh(mesh.devices.reshape(4, 2, 4, 8, 2), ("x", "y_hi", "y_lo", "z", "core"))
    tokens = P(SPAN, CHIPS + ("core",), None)
    return jax.shard_map(
        on_device,
        mesh=parts,
        in_specs=(tokens, tokens, tokens, P(), P(), P()),
        out_specs=tokens,
        check_vma=False,
    )
```

```python
import math

import jax
import jax.numpy as jnp
import numpy as np
from jax import lax
from jax.experimental import pallas as pl
from jax.experimental.pallas import tpu as pltpu
from jax.sharding import Mesh
from jax.sharding import PartitionSpec as P

HD = 128
SPAN = ("x", "y_hi")
CHIPS = ("y_lo", "z")
AXES = SPAN + CHIPS + ("core",)
CONST = HD ** (-0.5) * 1.4426950408889634
TILE = 384
VMEM_LIMIT = 24 * 1024 * 1024


def weigh(q, halves, top, const):
    dims = (((1,), (1,)), ((), ()))
    scores = [lax.dot_general(q, ref[0], dims, preferred_element_type=jnp.float32) for ref in halves]
    own = jnp.maximum(scores[0].max(axis=1, keepdims=True), scores[1].max(axis=1, keepdims=True))
    top, less = top(own)
    expos = [jnp.exp2((s - less) * const) for s in scores]
    total = expos[0].sum(axis=1, keepdims=True) + expos[1].sum(axis=1, keepdims=True)
    heard = sum(
        jnp.dot(e.astype(jnp.bfloat16), ref[1], preferred_element_type=jnp.float32)
        for e, ref in zip(expos, halves)
    )
    return top, total, heard


def diagonal():
    return lax.broadcasted_iota(jnp.int32, (HD, HD), 0) == lax.broadcasted_iota(jnp.int32, (HD, HD), 1)


def own_block(mask_ref, level_ref, gate_ref, q_ref, kv_ref, m_out, l_out, a_out, aux_out):
    span_at = lax.axis_index(SPAN)
    for distance in (1, 2):
        column = span_at - distance
        usable = jnp.logical_and(column >= 0, mask_ref[span_at, jnp.maximum(column, 0)] > 0)
        value = jnp.where(usable, 1.0, 0.0).astype(jnp.float32)
        aux_out[pl.ds((distance - 1) * 8, 8), :] = jnp.full((8, HD), value, jnp.float32)
    line, depth = lax.axis_size("y_lo"), lax.axis_size("z")
    at_line = lax.axis_index("y_lo")
    at_line = jnp.where(lax.axis_index("y_hi") > 0, line - 1 - at_line, at_line)
    head = at_line * depth + lax.axis_index("z")
    mine = gate_ref[:, pl.ds(pl.multiple_of(head * HD, HD), HD)]
    chosen = lax.broadcasted_iota(jnp.int32, mine.shape, 0) == level_ref[span_at]
    gate = jnp.where(chosen, mine, 0.0).sum(axis=0, keepdims=True)
    aux_out[pl.ds(16, 8), :] = jnp.broadcast_to(gate, (8, HD))
    for t in range(q_ref.shape[0] // TILE):
        at = pl.ds(t * TILE, TILE)
        top, total, heard = weigh(q_ref[at, :], (kv_ref.at[0], kv_ref.at[1]), lambda own: (own, own), CONST)
        m_out[at, :] = jnp.broadcast_to(top, (TILE, HD))
        l_out[at, :] = jnp.broadcast_to(total, (TILE, HD))
        a_out[at, :] = heard


def served_block(q_ref, kv_ref, out_ref):
    rows = q_ref.shape[0]
    eye = diagonal()
    stats = []
    for t in range(rows // TILE):
        at = pl.ds(t * TILE, TILE)
        top, total, heard = weigh(q_ref[at, :], (kv_ref.at[0], kv_ref.at[1]), lambda own: (own, own), CONST)
        out_ref[at, :] = (heard / total).astype(jnp.bfloat16)
        level = top + jnp.log2(total) * (1.0 / CONST)
        for j in range(TILE // HD):
            stats.append(jnp.where(eye, level[j * HD : (j + 1) * HD], 0.0).sum(axis=0, keepdims=True))
    spare = 8 - len(stats)
    level = jnp.concatenate(stats + [jnp.zeros((spare, HD), jnp.float32)], axis=0)
    high = level.astype(jnp.bfloat16).astype(jnp.float32)
    middle = (level - high).astype(jnp.bfloat16).astype(jnp.float32)
    low = level - high - middle
    pieces = jnp.concatenate((high, middle, low, jnp.zeros((8, HD), jnp.float32)), axis=0)
    out_ref[pl.ds(rows, 32), :] = pieces.astype(jnp.bfloat16)


def earlier_block(aux_ref, q_ref, kv_ref, m_in, l_in, a_in, m_out, l_out, a_out):
    opened = aux_ref[0:1, :1] > 0.5
    for t in range(q_ref.shape[0] // TILE):
        at = pl.ds(t * TILE, TILE)
        before = m_in[at, :1]

        def joined(own):
            top = jnp.where(opened, jnp.maximum(own, before), before)
            return top, jnp.where(opened, top, 1e30)

        top, total, heard = weigh(q_ref[at, :], (kv_ref.at[0], kv_ref.at[1]), joined, CONST)
        shrink = jnp.exp2((before - top) * CONST)
        m_out[at, :] = jnp.broadcast_to(top, (TILE, HD))
        l_out[at, :] = jnp.broadcast_to(total + l_in[at, :1] * shrink, (TILE, HD))
        a_out[at, :] = heard + a_in[at, :] * shrink


def join(aux_ref, m_in, l_in, a_in, part_ref, out_ref):
    rows = m_in.shape[0]
    opened = aux_ref[8:9, :1] > 0.5
    gate = aux_ref[16:17, :]
    eye = diagonal()
    pieces = part_ref[pl.ds(rows, 32), :].astype(jnp.float32)
    level = pieces[0:8] + pieces[8:16] + pieces[16:24]
    for t in range(rows // HD):
        at = pl.ds(t * HD, HD)
        before = m_in[at, :]
        served = jnp.where(eye, level[t : t + 1], 0.0).sum(axis=1, keepdims=True)
        served = jnp.where(opened, served, before)
        top = jnp.maximum(before, served)
        shrink = jnp.exp2((before - top) * CONST)
        share = jnp.where(opened, jnp.exp2((served - top) * CONST), 0.0)
        total = l_in[at, :] * shrink + share
        heard = a_in[at, :] * shrink + part_ref[at, :].astype(jnp.float32) * share
        out_ref[at, :] = (heard / total * gate).astype(jnp.bfloat16)


def split_heads(q_hbm, k_hbm, v_hbm, out_ref, *held_and_sems):
    held, sems = held_and_sems[:3], held_and_sems[3:]
    copies = [
        pltpu.make_async_copy(source, target, sem)
        for source, target, sem in zip((q_hbm, k_hbm, v_hbm), held, sems)
    ]
    for copy in copies:
        copy.start()
    for i, (copy, ref) in enumerate(zip(copies, held)):
        copy.wait()
        for h in range(out_ref.shape[0]):
            out_ref[h, i] = ref[0, :, h * HD : (h + 1) * HD]


def call(kernel, out_shape, scalars, *arrays):
    vmem = pl.BlockSpec(memory_space=pltpu.VMEM)
    smem = pl.BlockSpec(memory_space=pltpu.SMEM)
    return pl.pallas_call(
        kernel,
        out_shape=out_shape,
        in_specs=[smem] * len(scalars) + [vmem] * len(arrays),
        out_specs=[vmem] * len(out_shape),
        compiler_params=pltpu.CompilerParams(vmem_limit_bytes=VMEM_LIMIT),
        cost_estimate=pl.CostEstimate(flops=1024, bytes_accessed=1024, transcendentals=0),
    )(*scalars, *arrays)


def on_device(queries, key_rows, value_rows, block_mask, noise_level, gate_table):
    local = queries.shape[1]
    heads = queries.shape[2] // HD
    spans = lax.axis_size(SPAN)
    rows = heads * local

    sizes = [lax.axis_size(axis) for axis in AXES]
    line = sizes[2]
    number = np.arange(math.prod(sizes)).reshape(sizes)
    number[:, 1] = number[:, 1, ::-1].copy()
    groups = number.transpose(0, 1, 4, 2, 3).reshape(-1, heads).tolist()

    def to_next(block):
        route = []
        for at, index in enumerate(np.ndindex(spans, line)):
            if index[0] + 1 < spans:
                route.append((at, (index[0] + 1) * line + line - 1 - index[1]))
        return lax.ppermute(block, SPAN + ("y_lo",), route)

    def exchange(block):
        return lax.all_to_all(
            block, AXES, split_axis=0, concat_axis=0, axis_index_groups=groups, tiled=True
        )

    def moved(block, distance):
        route = [(i, i + distance) for i in range(spans) if 0 <= i + distance < spans]
        return lax.ppermute(block, SPAN, route)

    def other_core(block):
        return lax.ppermute(block, "core", [(0, 1), (1, 0)])

    def both_cores(block):
        return lax.all_gather(block, "core")

    by_head = jax.ShapeDtypeStruct((heads, 3, local, HD), queries.dtype)
    mixed = pl.pallas_call(
        split_heads,
        out_shape=by_head,
        in_specs=[pl.BlockSpec(memory_space=pltpu.HBM)] * 3,
        out_specs=pl.BlockSpec(memory_space=pltpu.VMEM),
        scratch_shapes=[pltpu.VMEM(queries.shape, queries.dtype)] * 3 + [pltpu.SemaphoreType.DMA] * 3,
        compiler_params=pltpu.CompilerParams(vmem_limit_bytes=VMEM_LIMIT),
    )(queries, key_rows, value_rows)
    got = exchange(mixed)
    q = got[:, 0].reshape(rows, HD)
    kv = got[:, 1:].transpose(1, 0, 2, 3).reshape(2, rows, HD)

    stat = jax.ShapeDtypeStruct((rows, HD), jnp.float32)
    aux = jax.ShapeDtypeStruct((24, HD), jnp.float32)
    part = jax.ShapeDtypeStruct((rows + 32, HD), jnp.bfloat16)
    kv1 = to_next(kv)
    later_q = moved(q, -2)
    kv0 = both_cores(kv)
    *state, aux = call(own_block, [stat, stat, stat, aux], (block_mask, noise_level), gate_table, q, kv0)
    later_q, *state = lax.optimization_barrier((later_q, *state))
    (served,) = call(served_block, [part], (), later_q, kv0)
    part2 = moved(served, 2)
    kv1 = both_cores(kv1)
    state = call(earlier_block, [stat, stat, stat], (), aux, q, kv1, *state)
    (out,) = call(join, [jax.ShapeDtypeStruct((rows, HD), jnp.bfloat16)], (), aux, *state, part2)

    back = exchange(out.reshape(heads, local, HD))
    return back.transpose(1, 0, 2).reshape(1, local, heads * HD)


def solution(mesh):
    parts = Mesh(mesh.devices.reshape(4, 2, 4, 8, 2), ("x", "y_hi", "y_lo", "z", "core"))
    tokens = P(SPAN, CHIPS + ("core",), None)
    return jax.shard_map(
        on_device,
        mesh=parts,
        in_specs=(tokens, tokens, tokens, P(), P(), P()),
        out_specs=tokens,
        check_vma=False,
    )
```

```python
import jax
import jax.numpy as jnp
import numpy as np
from jax import lax
from jax.experimental import pallas as pl
from jax.experimental.pallas import tpu as pltpu
from jax.sharding import Mesh
from jax.sharding import PartitionSpec as P

HD = 128
SPAN = ("x", "y_hi")
CHIPS = ("y_lo", "z")
CONST = HD ** (-0.5) * 1.4426950408889634
TILE = 384
VMEM_LIMIT = 24 * 1024 * 1024


def weigh(q, halves, top, const):
    dims = (((1,), (1,)), ((), ()))
    scores = [lax.dot_general(q, ref[0], dims, preferred_element_type=jnp.float32) for ref in halves]
    own = jnp.maximum(scores[0].max(axis=1, keepdims=True), scores[1].max(axis=1, keepdims=True))
    top, less = top(own)
    expos = [jnp.exp2((s - less) * const) for s in scores]
    total = expos[0].sum(axis=1, keepdims=True) + expos[1].sum(axis=1, keepdims=True)
    heard = sum(
        jnp.dot(e.astype(jnp.bfloat16), ref[1], preferred_element_type=jnp.float32)
        for e, ref in zip(expos, halves)
    )
    return top, total, heard


def diagonal():
    return lax.broadcasted_iota(jnp.int32, (HD, HD), 0) == lax.broadcasted_iota(jnp.int32, (HD, HD), 1)


def own_block(mask_ref, level_ref, gate_ref, q_ref, kv_ref, m_out, l_out, a_out, aux_out):
    span_at = lax.axis_index(SPAN)
    for distance in (1, 2):
        column = span_at - distance
        usable = jnp.logical_and(column >= 0, mask_ref[span_at, jnp.maximum(column, 0)] > 0)
        value = jnp.where(usable, 1.0, 0.0).astype(jnp.float32)
        aux_out[pl.ds((distance - 1) * 8, 8), :] = jnp.full((8, HD), value, jnp.float32)
    head = placed(lax.axis_index("y_lo") * lax.axis_size("z") + lax.axis_index("z"))
    mine = gate_ref[:, pl.ds(pl.multiple_of(head * HD, HD), HD)]
    chosen = lax.broadcasted_iota(jnp.int32, mine.shape, 0) == level_ref[span_at]
    gate = jnp.where(chosen, mine, 0.0).sum(axis=0, keepdims=True)
    aux_out[pl.ds(16, 8), :] = jnp.broadcast_to(gate, (8, HD))
    for t in range(q_ref.shape[0] // TILE):
        at = pl.ds(t * TILE, TILE)
        top, total, heard = weigh(q_ref[at, :], (kv_ref.at[0], kv_ref.at[1]), lambda own: (own, own), CONST)
        m_out[at, :] = jnp.broadcast_to(top, (TILE, HD))
        l_out[at, :] = jnp.broadcast_to(total, (TILE, HD))
        a_out[at, :] = heard


def served_block(q_ref, kv_ref, out_ref):
    rows = q_ref.shape[0]
    eye = diagonal()
    stats = []
    for t in range(rows // TILE):
        at = pl.ds(t * TILE, TILE)
        top, total, heard = weigh(q_ref[at, :], (kv_ref.at[0], kv_ref.at[1]), lambda own: (own, own), CONST)
        out_ref[at, :] = (heard / total).astype(jnp.bfloat16)
        level = top + jnp.log2(total) * (1.0 / CONST)
        for j in range(TILE // HD):
            stats.append(jnp.where(eye, level[j * HD : (j + 1) * HD], 0.0).sum(axis=0, keepdims=True))
    spare = 8 - len(stats)
    level = jnp.concatenate(stats + [jnp.zeros((spare, HD), jnp.float32)], axis=0)
    high = level.astype(jnp.bfloat16).astype(jnp.float32)
    middle = (level - high).astype(jnp.bfloat16).astype(jnp.float32)
    low = level - high - middle
    pieces = jnp.concatenate((high, middle, low, jnp.zeros((8, HD), jnp.float32)), axis=0)
    out_ref[pl.ds(rows, 32), :] = pieces.astype(jnp.bfloat16)


def earlier_block(aux_ref, q_ref, kv_ref, m_in, l_in, a_in, m_out, l_out, a_out):
    opened = aux_ref[0:1, :1] > 0.5
    for t in range(q_ref.shape[0] // TILE):
        at = pl.ds(t * TILE, TILE)
        before = m_in[at, :1]

        def joined(own):
            top = jnp.where(opened, jnp.maximum(own, before), before)
            return top, jnp.where(opened, top, 1e30)

        top, total, heard = weigh(q_ref[at, :], (kv_ref.at[0], kv_ref.at[1]), joined, CONST)
        shrink = jnp.exp2((before - top) * CONST)
        m_out[at, :] = jnp.broadcast_to(top, (TILE, HD))
        l_out[at, :] = jnp.broadcast_to(total + l_in[at, :1] * shrink, (TILE, HD))
        a_out[at, :] = heard + a_in[at, :] * shrink


def join(aux_ref, m_in, l_in, a_in, part_ref, out_ref):
    rows = m_in.shape[0]
    opened = aux_ref[8:9, :1] > 0.5
    gate = aux_ref[16:17, :]
    eye = diagonal()
    pieces = part_ref[pl.ds(rows, 32), :].astype(jnp.float32)
    level = pieces[0:8] + pieces[8:16] + pieces[16:24]
    for t in range(rows // HD):
        at = pl.ds(t * HD, HD)
        before = m_in[at, :]
        served = jnp.where(eye, level[t : t + 1], 0.0).sum(axis=1, keepdims=True)
        served = jnp.where(opened, served, before)
        top = jnp.maximum(before, served)
        shrink = jnp.exp2((before - top) * CONST)
        share = jnp.where(opened, jnp.exp2((served - top) * CONST), 0.0)
        total = l_in[at, :] * shrink + share
        heard = a_in[at, :] * shrink + part_ref[at, :].astype(jnp.float32) * share
        out_ref[at, :] = (heard / total * gate).astype(jnp.bfloat16)


def placed(index):
    line, depth = lax.axis_size("y_lo"), lax.axis_size("z")
    at, z = index // depth, index % depth
    return jnp.where(lax.axis_index("y_hi") > 0, line - 1 - at, at) * depth + z


def split_heads(q_hbm, k_hbm, v_hbm, out_ref, *held_and_sems):
    held, sems = held_and_sems[:3], held_and_sems[3:]
    copies = [
        pltpu.make_async_copy(source, target, sem)
        for source, target, sem in zip((q_hbm, k_hbm, v_hbm), held, sems)
    ]
    for copy in copies:
        copy.start()
    for i, (copy, ref) in enumerate(zip(copies, held)):
        copy.wait()
        for h in range(out_ref.shape[0]):
            out_ref[placed(h), i] = ref[0, :, h * HD : (h + 1) * HD]


def join_heads(in_ref, out_ref):
    for h in range(in_ref.shape[0]):
        out_ref[0, :, h * HD : (h + 1) * HD] = in_ref[placed(h)]


def call(kernel, out_shape, scalars, *arrays):
    vmem = pl.BlockSpec(memory_space=pltpu.VMEM)
    smem = pl.BlockSpec(memory_space=pltpu.SMEM)
    return pl.pallas_call(
        kernel,
        out_shape=out_shape,
        in_specs=[smem] * len(scalars) + [vmem] * len(arrays),
        out_specs=[vmem] * len(out_shape),
        compiler_params=pltpu.CompilerParams(vmem_limit_bytes=VMEM_LIMIT),
        cost_estimate=pl.CostEstimate(flops=1024, bytes_accessed=1024, transcendentals=0),
    )(*scalars, *arrays)


def on_device(queries, key_rows, value_rows, block_mask, noise_level, gate_table):
    local = queries.shape[1]
    heads = queries.shape[2] // HD
    spans = lax.axis_size(SPAN)
    rows = heads * local

    line = lax.axis_size("y_lo")

    def to_next(block):
        route = []
        for at, index in enumerate(np.ndindex(spans, line)):
            if index[0] + 1 < spans:
                route.append((at, (index[0] + 1) * line + line - 1 - index[1]))
        return lax.ppermute(block, SPAN + ("y_lo",), route)

    def exchange(block):
        return lax.all_to_all(block, CHIPS, split_axis=0, concat_axis=0, tiled=True)

    def moved(block, distance):
        route = [(i, i + distance) for i in range(spans) if 0 <= i + distance < spans]
        return lax.ppermute(block, SPAN, route)

    def other_core(block):
        return lax.ppermute(block, "core", [(0, 1), (1, 0)])

    def both_cores(block):
        return lax.all_gather(block, "core")

    by_head = jax.ShapeDtypeStruct((heads, 3, local, HD), queries.dtype)
    mixed = pl.pallas_call(
        split_heads,
        out_shape=by_head,
        in_specs=[pl.BlockSpec(memory_space=pltpu.HBM)] * 3,
        out_specs=pl.BlockSpec(memory_space=pltpu.VMEM),
        scratch_shapes=[pltpu.VMEM(queries.shape, queries.dtype)] * 3 + [pltpu.SemaphoreType.DMA] * 3,
        compiler_params=pltpu.CompilerParams(vmem_limit_bytes=60 * 1024 * 1024),
    )(queries, key_rows, value_rows)
    got = exchange(mixed)
    q = got[:, 0].reshape(rows, HD)
    kv = got[:, 1:].transpose(1, 0, 2, 3).reshape(2, rows, HD)

    stat = jax.ShapeDtypeStruct((rows, HD), jnp.float32)
    aux = jax.ShapeDtypeStruct((24, HD), jnp.float32)
    part = jax.ShapeDtypeStruct((rows + 32, HD), jnp.bfloat16)
    kv1 = to_next(kv)
    later_q = moved(q, -2)
    kv0 = both_cores(kv)
    *state, aux = call(own_block, [stat, stat, stat, aux], (block_mask, noise_level), gate_table, q, kv0)
    later_q, *state = lax.optimization_barrier((later_q, *state))
    (served,) = call(served_block, [part], (), later_q, kv0)
    part2 = moved(served, 2)
    kv1 = both_cores(kv1)
    state = call(earlier_block, [stat, stat, stat], (), aux, q, kv1, *state)
    (out,) = call(join, [jax.ShapeDtypeStruct((rows, HD), jnp.bfloat16)], (), aux, *state, part2)

    back = exchange(out.reshape(heads, local, HD))
    (attended,) = call(join_heads, [jax.ShapeDtypeStruct(queries.shape, queries.dtype)], (), back)
    return attended


def solution(mesh):
    parts = Mesh(mesh.devices.reshape(4, 2, 4, 8, 2), ("x", "y_hi", "y_lo", "z", "core"))
    tokens = P(SPAN, CHIPS + ("core",), None)
    return jax.shard_map(
        on_device,
        mesh=parts,
        in_specs=(tokens, tokens, tokens, P(), P(), P()),
        out_specs=tokens,
        check_vma=False,
    )
```

```python
import jax
import jax.numpy as jnp
import numpy as np
from jax import lax
from jax.experimental import pallas as pl
from jax.experimental.pallas import tpu as pltpu
from jax.sharding import Mesh
from jax.sharding import PartitionSpec as P

HD = 128
SPAN = ("x", "y_hi")
CHIPS = ("y_lo", "z")
CONST = HD ** (-0.5) * 1.4426950408889634
TILE = 384
CHUNKS = 4
VMEM_LIMIT = 24 * 1024 * 1024


def weigh(q, halves, top, const):
    dims = (((1,), (1,)), ((), ()))
    scores = [lax.dot_general(q, ref[0], dims, preferred_element_type=jnp.float32) for ref in halves]
    own = jnp.maximum(scores[0].max(axis=1, keepdims=True), scores[1].max(axis=1, keepdims=True))
    top, less = top(own)
    expos = [jnp.exp2((s - less) * const) for s in scores]
    total = expos[0].sum(axis=1, keepdims=True) + expos[1].sum(axis=1, keepdims=True)
    heard = sum(
        jnp.dot(e.astype(jnp.bfloat16), ref[1], preferred_element_type=jnp.float32)
        for e, ref in zip(expos, halves)
    )
    return top, total, heard


def diagonal():
    return lax.broadcasted_iota(jnp.int32, (HD, HD), 0) == lax.broadcasted_iota(jnp.int32, (HD, HD), 1)


def own_block(mask_ref, level_ref, gate_ref, q_ref, kv_ref, m_out, l_out, a_out, aux_out):
    span_at = lax.axis_index(SPAN)
    for distance in (1, 2):
        column = span_at - distance
        usable = jnp.logical_and(column >= 0, mask_ref[span_at, jnp.maximum(column, 0)] > 0)
        value = jnp.where(usable, 1.0, 0.0).astype(jnp.float32)
        aux_out[pl.ds((distance - 1) * 8, 8), :] = jnp.full((8, HD), value, jnp.float32)
    head = placed(lax.axis_index("y_lo") * lax.axis_size("z") + lax.axis_index("z"))
    mine = gate_ref[:, pl.ds(pl.multiple_of(head * HD, HD), HD)]
    chosen = lax.broadcasted_iota(jnp.int32, mine.shape, 0) == level_ref[span_at]
    gate = jnp.where(chosen, mine, 0.0).sum(axis=0, keepdims=True)
    aux_out[pl.ds(16, 8), :] = jnp.broadcast_to(gate, (8, HD))
    for t in range(q_ref.shape[0] // TILE):
        at = pl.ds(t * TILE, TILE)
        top, total, heard = weigh(q_ref[at, :], (kv_ref.at[0], kv_ref.at[1]), lambda own: (own, own), CONST)
        m_out[at, :] = jnp.broadcast_to(top, (TILE, HD))
        l_out[at, :] = jnp.broadcast_to(total, (TILE, HD))
        a_out[at, :] = heard


def served_block(q_ref, kv_ref, out_ref):
    rows = q_ref.shape[0]
    eye = diagonal()
    stats = []
    for t in range(rows // TILE):
        at = pl.ds(t * TILE, TILE)
        top, total, heard = weigh(q_ref[at, :], (kv_ref.at[0], kv_ref.at[1]), lambda own: (own, own), CONST)
        out_ref[at, :] = (heard / total).astype(jnp.bfloat16)
        level = top + jnp.log2(total) * (1.0 / CONST)
        for j in range(TILE // HD):
            stats.append(jnp.where(eye, level[j * HD : (j + 1) * HD], 0.0).sum(axis=0, keepdims=True))
    spare = 8 - len(stats)
    level = jnp.concatenate(stats + [jnp.zeros((spare, HD), jnp.float32)], axis=0)
    high = level.astype(jnp.bfloat16).astype(jnp.float32)
    middle = (level - high).astype(jnp.bfloat16).astype(jnp.float32)
    low = level - high - middle
    pieces = jnp.concatenate((high, middle, low, jnp.zeros((8, HD), jnp.float32)), axis=0)
    out_ref[pl.ds(rows, 32), :] = pieces.astype(jnp.bfloat16)


def earlier_block(aux_ref, q_ref, kv_ref, m_in, l_in, a_in, m_out, l_out, a_out):
    opened = aux_ref[0:1, :1] > 0.5
    for t in range(q_ref.shape[0] // TILE):
        at = pl.ds(t * TILE, TILE)
        before = m_in[at, :1]

        def joined(own):
            top = jnp.where(opened, jnp.maximum(own, before), before)
            return top, jnp.where(opened, top, 1e30)

        top, total, heard = weigh(q_ref[at, :], (kv_ref.at[0], kv_ref.at[1]), joined, CONST)
        shrink = jnp.exp2((before - top) * CONST)
        m_out[at, :] = jnp.broadcast_to(top, (TILE, HD))
        l_out[at, :] = jnp.broadcast_to(total + l_in[at, :1] * shrink, (TILE, HD))
        a_out[at, :] = heard + a_in[at, :] * shrink


def join(aux_ref, m_in, l_in, a_in, part_ref, out_ref):
    rows = m_in.shape[0]
    opened = aux_ref[8:9, :1] > 0.5
    gate = aux_ref[16:17, :]
    eye = diagonal()
    pieces = part_ref[pl.ds(rows, 32), :].astype(jnp.float32)
    level = pieces[0:8] + pieces[8:16] + pieces[16:24]
    for t in range(rows // HD):
        at = pl.ds(t * HD, HD)
        before = m_in[at, :]
        served = jnp.where(eye, level[t : t + 1], 0.0).sum(axis=1, keepdims=True)
        served = jnp.where(opened, served, before)
        top = jnp.maximum(before, served)
        shrink = jnp.exp2((before - top) * CONST)
        share = jnp.where(opened, jnp.exp2((served - top) * CONST), 0.0)
        total = l_in[at, :] * shrink + share
        heard = a_in[at, :] * shrink + part_ref[at, :].astype(jnp.float32) * share
        out_ref[at, :] = (heard / total * gate).astype(jnp.bfloat16)


def placed(index):
    line, depth = lax.axis_size("y_lo"), lax.axis_size("z")
    at, z = index // depth, index % depth
    return jnp.where(lax.axis_index("y_hi") > 0, line - 1 - at, at) * depth + z


def split_heads(q_hbm, k_hbm, v_hbm, out_ref, held, sems):
    wide = q_hbm.shape[2] // CHUNKS
    copies = []
    for i, source in enumerate((q_hbm, k_hbm, v_hbm)):
        for c in range(CHUNKS):
            at = pl.ds(c * wide, wide)
            copies.append(
                pltpu.make_async_copy(source.at[0, :, at], held.at[i, :, at], sems.at[i * CHUNKS + c])
            )
    for copy in copies:
        copy.start()
    each = out_ref.shape[0] // CHUNKS
    for i in range(3):
        for c in range(CHUNKS):
            copies[i * CHUNKS + c].wait()
            for h in range(c * each, (c + 1) * each):
                out_ref[placed(h), i] = held[i, :, h * HD : (h + 1) * HD]


def join_heads(in_ref, out_hbm, held, sems):
    each = in_ref.shape[0] // CHUNKS
    copies = []
    for c in range(CHUNKS):
        for h in range(c * each, (c + 1) * each):
            held[:, h * HD : (h + 1) * HD] = in_ref[placed(h)]
        at = pl.ds(c * each * HD, each * HD)
        copies.append(pltpu.make_async_copy(held.at[:, at], out_hbm.at[0, :, at], sems.at[c]))
        copies[-1].start()
    for copy in copies:
        copy.wait()


def call(kernel, out_shape, scalars, *arrays):
    vmem = pl.BlockSpec(memory_space=pltpu.VMEM)
    smem = pl.BlockSpec(memory_space=pltpu.SMEM)
    return pl.pallas_call(
        kernel,
        out_shape=out_shape,
        in_specs=[smem] * len(scalars) + [vmem] * len(arrays),
        out_specs=[vmem] * len(out_shape),
        compiler_params=pltpu.CompilerParams(vmem_limit_bytes=VMEM_LIMIT),
        cost_estimate=pl.CostEstimate(flops=1024, bytes_accessed=1024, transcendentals=0),
    )(*scalars, *arrays)


def on_device(queries, key_rows, value_rows, block_mask, noise_level, gate_table):
    local = queries.shape[1]
    heads = queries.shape[2] // HD
    spans = lax.axis_size(SPAN)
    rows = heads * local

    line = lax.axis_size("y_lo")

    def to_next(block):
        route = []
        for at, index in enumerate(np.ndindex(spans, line)):
            if index[0] + 1 < spans:
                route.append((at, (index[0] + 1) * line + line - 1 - index[1]))
        return lax.ppermute(block, SPAN + ("y_lo",), route)

    def exchange(block):
        return lax.all_to_all(block, CHIPS, split_axis=0, concat_axis=0, tiled=True)

    def moved(block, distance):
        route = [(i, i + distance) for i in range(spans) if 0 <= i + distance < spans]
        return lax.ppermute(block, SPAN, route)

    def other_core(block):
        return lax.ppermute(block, "core", [(0, 1), (1, 0)])

    def both_cores(block):
        return lax.all_gather(block, "core")

    by_head = jax.ShapeDtypeStruct((heads, 3, local, HD), queries.dtype)
    mixed = pl.pallas_call(
        split_heads,
        out_shape=by_head,
        in_specs=[pl.BlockSpec(memory_space=pltpu.HBM)] * 3,
        out_specs=pl.BlockSpec(memory_space=pltpu.VMEM),
        scratch_shapes=[
            pltpu.VMEM((3, local, heads * HD), queries.dtype),
            pltpu.SemaphoreType.DMA((3 * CHUNKS,)),
        ],
        compiler_params=pltpu.CompilerParams(vmem_limit_bytes=60 * 1024 * 1024),
    )(queries, key_rows, value_rows)
    got = exchange(mixed)
    q = got[:, 0].reshape(rows, HD)
    kv = got[:, 1:].transpose(1, 0, 2, 3).reshape(2, rows, HD)

    stat = jax.ShapeDtypeStruct((rows, HD), jnp.float32)
    aux = jax.ShapeDtypeStruct((24, HD), jnp.float32)
    part = jax.ShapeDtypeStruct((rows + 32, HD), jnp.bfloat16)
    kv1 = to_next(kv)
    later_q = moved(q, -2)
    kv0 = both_cores(kv)
    (served,) = call(served_block, [part], (), later_q, kv0)
    *state, aux = call(own_block, [stat, stat, stat, aux], (block_mask, noise_level), gate_table, q, kv0)
    part2 = moved(served, 2)
    kv1 = both_cores(kv1)
    state = call(earlier_block, [stat, stat, stat], (), aux, q, kv1, *state)
    (out,) = call(join, [jax.ShapeDtypeStruct((rows, HD), jnp.bfloat16)], (), aux, *state, part2)

    back = exchange(out.reshape(heads, local, HD))
    return pl.pallas_call(
        join_heads,
        out_shape=jax.ShapeDtypeStruct(queries.shape, queries.dtype),
        in_specs=[pl.BlockSpec(memory_space=pltpu.VMEM)],
        out_specs=pl.BlockSpec(memory_space=pltpu.HBM),
        scratch_shapes=[pltpu.VMEM((local, heads * HD), queries.dtype), pltpu.SemaphoreType.DMA((CHUNKS,))],
        compiler_params=pltpu.CompilerParams(vmem_limit_bytes=VMEM_LIMIT),
    )(back)


def solution(mesh):
    parts = Mesh(mesh.devices.reshape(4, 2, 4, 8, 2), ("x", "y_hi", "y_lo", "z", "core"))
    tokens = P(SPAN, CHIPS + ("core",), None)
    return jax.shard_map(
        on_device,
        mesh=parts,
        in_specs=(tokens, tokens, tokens, P(), P(), P()),
        out_specs=tokens,
        check_vma=False,
    )
```

```python
import jax
import jax.numpy as jnp
import numpy as np
from jax import lax
from jax.experimental import pallas as pl
from jax.experimental.pallas import tpu as pltpu
from jax.sharding import Mesh
from jax.sharding import PartitionSpec as P

HD = 128
SPAN = ("x", "y_hi")
CHIPS = ("y_lo", "z")
CONST = HD ** (-0.5) * 1.4426950408889634
TILE = 384
CHUNKS = 4
VMEM_LIMIT = 24 * 1024 * 1024


def weigh(q, halves, top, const):
    dims = (((1,), (1,)), ((), ()))
    scores = [lax.dot_general(q, ref[0], dims, preferred_element_type=jnp.float32) for ref in halves]
    own = jnp.maximum(scores[0].max(axis=1, keepdims=True), scores[1].max(axis=1, keepdims=True))
    top, less = top(own)
    expos = [jnp.exp2((s - less) * const) for s in scores]
    total = expos[0].sum(axis=1, keepdims=True) + expos[1].sum(axis=1, keepdims=True)
    heard = sum(
        jnp.dot(e.astype(jnp.bfloat16), ref[1], preferred_element_type=jnp.float32)
        for e, ref in zip(expos, halves)
    )
    return top, total, heard


def diagonal():
    return lax.broadcasted_iota(jnp.int32, (HD, HD), 0) == lax.broadcasted_iota(jnp.int32, (HD, HD), 1)


def own_block(mask_ref, level_ref, gate_ref, q_ref, kv_ref, m_out, l_out, a_out, aux_out):
    span_at = lax.axis_index(SPAN)
    for distance in (1, 2):
        column = span_at - distance
        usable = jnp.logical_and(column >= 0, mask_ref[span_at, jnp.maximum(column, 0)] > 0)
        value = jnp.where(usable, 1.0, 0.0).astype(jnp.float32)
        aux_out[pl.ds((distance - 1) * 8, 8), :] = jnp.full((8, HD), value, jnp.float32)
    head = placed(lax.axis_index("y_lo") * lax.axis_size("z") + lax.axis_index("z"))
    mine = gate_ref[:, pl.ds(pl.multiple_of(head * HD, HD), HD)]
    chosen = lax.broadcasted_iota(jnp.int32, mine.shape, 0) == level_ref[span_at]
    gate = jnp.where(chosen, mine, 0.0).sum(axis=0, keepdims=True)
    aux_out[pl.ds(16, 8), :] = jnp.broadcast_to(gate, (8, HD))
    for t in range(q_ref.shape[0] // TILE):
        at = pl.ds(t * TILE, TILE)
        top, total, heard = weigh(q_ref[at, :], (kv_ref.at[0], kv_ref.at[1]), lambda own: (own, own), CONST)
        m_out[at, :] = jnp.broadcast_to(top, (TILE, HD))
        l_out[at, :] = jnp.broadcast_to(total, (TILE, HD))
        a_out[at, :] = heard


def served_block(q_ref, kv_ref, out_ref):
    rows = q_ref.shape[0]
    eye = diagonal()
    stats = []
    for t in range(rows // TILE):
        at = pl.ds(t * TILE, TILE)
        top, total, heard = weigh(q_ref[at, :], (kv_ref.at[0], kv_ref.at[1]), lambda own: (own, own), CONST)
        out_ref[at, :] = (heard / total).astype(jnp.bfloat16)
        level = top + jnp.log2(total) * (1.0 / CONST)
        for j in range(TILE // HD):
            stats.append(jnp.where(eye, level[j * HD : (j + 1) * HD], 0.0).sum(axis=0, keepdims=True))
    spare = 8 - len(stats)
    level = jnp.concatenate(stats + [jnp.zeros((spare, HD), jnp.float32)], axis=0)
    high = level.astype(jnp.bfloat16).astype(jnp.float32)
    middle = (level - high).astype(jnp.bfloat16).astype(jnp.float32)
    low = level - high - middle
    pieces = jnp.concatenate((high, middle, low, jnp.zeros((8, HD), jnp.float32)), axis=0)
    out_ref[pl.ds(rows, 32), :] = pieces.astype(jnp.bfloat16)


def last_block(aux_ref, q_ref, kv_ref, m_in, l_in, a_in, part_ref, out_ref):
    rows = q_ref.shape[0]
    opened1 = aux_ref[0:1, :1] > 0.5
    opened2 = aux_ref[8:9, :1] > 0.5
    gate = aux_ref[16:17, :]
    eye = diagonal()
    pieces = part_ref[pl.ds(rows, 32), :].astype(jnp.float32)
    level = pieces[0:8] + pieces[8:16] + pieces[16:24]
    for t in range(rows // TILE):
        at = pl.ds(t * TILE, TILE)
        before = m_in[at, :1]
        served = jnp.concatenate(
            [
                jnp.where(eye, level[j : j + 1], 0.0).sum(axis=1, keepdims=True)
                for j in range(t * TILE // HD, (t + 1) * TILE // HD)
            ],
            axis=0,
        )
        known = jnp.where(opened2, jnp.maximum(before, served), before)

        def joined(own):
            top = jnp.where(opened1, jnp.maximum(own, known), known)
            return top, jnp.where(opened1, top, 1e30)

        top, total, heard = weigh(q_ref[at, :], (kv_ref.at[0], kv_ref.at[1]), joined, CONST)
        shrink = jnp.exp2((before - top) * CONST)
        share = jnp.where(opened2, jnp.exp2((jnp.where(opened2, served, top) - top) * CONST), 0.0)
        total = total + l_in[at, :1] * shrink + share
        heard = heard + a_in[at, :] * shrink + part_ref[at, :].astype(jnp.float32) * share
        out_ref[at, :] = (heard / total * gate).astype(jnp.bfloat16)


def placed(index):
    line, depth = lax.axis_size("y_lo"), lax.axis_size("z")
    at, z = index // depth, index % depth
    return jnp.where(lax.axis_index("y_hi") > 0, line - 1 - at, at) * depth + z


def split_heads(q_hbm, k_hbm, v_hbm, out_ref, held, sems):
    wide = q_hbm.shape[2] // CHUNKS
    copies = []
    for i, source in enumerate((q_hbm, k_hbm, v_hbm)):
        for c in range(CHUNKS):
            at = pl.ds(c * wide, wide)
            copies.append(
                pltpu.make_async_copy(source.at[0, :, at], held.at[i, :, at], sems.at[i * CHUNKS + c])
            )
    for copy in copies:
        copy.start()
    each = out_ref.shape[0] // CHUNKS
    for i in range(3):
        for c in range(CHUNKS):
            copies[i * CHUNKS + c].wait()
            for h in range(c * each, (c + 1) * each):
                out_ref[placed(h), i] = held[i, :, h * HD : (h + 1) * HD]


def join_heads(in_ref, out_hbm, held, sems):
    each = in_ref.shape[0] // CHUNKS
    copies = []
    for c in range(CHUNKS):
        for h in range(c * each, (c + 1) * each):
            held[:, h * HD : (h + 1) * HD] = in_ref[placed(h)]
        at = pl.ds(c * each * HD, each * HD)
        copies.append(pltpu.make_async_copy(held.at[:, at], out_hbm.at[0, :, at], sems.at[c]))
        copies[-1].start()
    for copy in copies:
        copy.wait()


def call(kernel, out_shape, scalars, *arrays):
    vmem = pl.BlockSpec(memory_space=pltpu.VMEM)
    smem = pl.BlockSpec(memory_space=pltpu.SMEM)
    return pl.pallas_call(
        kernel,
        out_shape=out_shape,
        in_specs=[smem] * len(scalars) + [vmem] * len(arrays),
        out_specs=[vmem] * len(out_shape),
        compiler_params=pltpu.CompilerParams(vmem_limit_bytes=VMEM_LIMIT),
        cost_estimate=pl.CostEstimate(flops=1024, bytes_accessed=1024, transcendentals=0),
    )(*scalars, *arrays)


def on_device(queries, key_rows, value_rows, block_mask, noise_level, gate_table):
    local = queries.shape[1]
    heads = queries.shape[2] // HD
    spans = lax.axis_size(SPAN)
    rows = heads * local

    line = lax.axis_size("y_lo")

    def to_next(block):
        route = []
        for at, index in enumerate(np.ndindex(spans, line)):
            if index[0] + 1 < spans:
                route.append((at, (index[0] + 1) * line + line - 1 - index[1]))
        return lax.ppermute(block, SPAN + ("y_lo",), route)

    def exchange(block):
        return lax.all_to_all(block, CHIPS, split_axis=0, concat_axis=0, tiled=True)

    def moved(block, distance):
        route = [(i, i + distance) for i in range(spans) if 0 <= i + distance < spans]
        return lax.ppermute(block, SPAN, route)

    def other_core(block):
        return lax.ppermute(block, "core", [(0, 1), (1, 0)])

    def both_cores(block):
        return lax.all_gather(block, "core")

    by_head = jax.ShapeDtypeStruct((heads, 3, local, HD), queries.dtype)
    mixed = pl.pallas_call(
        split_heads,
        out_shape=by_head,
        in_specs=[pl.BlockSpec(memory_space=pltpu.HBM)] * 3,
        out_specs=pl.BlockSpec(memory_space=pltpu.VMEM),
        scratch_shapes=[
            pltpu.VMEM((3, local, heads * HD), queries.dtype),
            pltpu.SemaphoreType.DMA((3 * CHUNKS,)),
        ],
        compiler_params=pltpu.CompilerParams(vmem_limit_bytes=60 * 1024 * 1024),
    )(queries, key_rows, value_rows)
    got = exchange(mixed)
    q = got[:, 0].reshape(rows, HD)
    kv = got[:, 1:].transpose(1, 0, 2, 3).reshape(2, rows, HD)

    stat = jax.ShapeDtypeStruct((rows, HD), jnp.float32)
    aux = jax.ShapeDtypeStruct((24, HD), jnp.float32)
    part = jax.ShapeDtypeStruct((rows + 32, HD), jnp.bfloat16)
    kv1 = to_next(kv)
    later_q = moved(q, -2)
    kv0 = both_cores(kv)
    (served,) = call(served_block, [part], (), later_q, kv0)
    *state, aux = call(own_block, [stat, stat, stat, aux], (block_mask, noise_level), gate_table, q, kv0)
    part2 = moved(served, 2)
    kv1 = both_cores(kv1)
    (out,) = call(
        last_block, [jax.ShapeDtypeStruct((rows, HD), jnp.bfloat16)], (), aux, q, kv1, *state, part2
    )

    back = exchange(out.reshape(heads, local, HD))
    return pl.pallas_call(
        join_heads,
        out_shape=jax.ShapeDtypeStruct(queries.shape, queries.dtype),
        in_specs=[pl.BlockSpec(memory_space=pltpu.VMEM)],
        out_specs=pl.BlockSpec(memory_space=pltpu.HBM),
        scratch_shapes=[pltpu.VMEM((local, heads * HD), queries.dtype), pltpu.SemaphoreType.DMA((CHUNKS,))],
        compiler_params=pltpu.CompilerParams(vmem_limit_bytes=VMEM_LIMIT),
    )(back)


def solution(mesh):
    parts = Mesh(mesh.devices.reshape(4, 2, 4, 8, 2), ("x", "y_hi", "y_lo", "z", "core"))
    tokens = P(SPAN, CHIPS + ("core",), None)
    return jax.shard_map(
        on_device,
        mesh=parts,
        in_specs=(tokens, tokens, tokens, P(), P(), P()),
        out_specs=tokens,
        check_vma=False,
    )
```

```python
import jax
import jax.numpy as jnp
import numpy as np
from jax import lax
from jax.experimental import pallas as pl
from jax.experimental.pallas import tpu as pltpu
from jax.sharding import Mesh
from jax.sharding import PartitionSpec as P

HD = 128
SPAN = ("x", "y_hi")
CHIPS = ("y_lo", "z")
CONST = HD ** (-0.5) * 1.4426950408889634
TILE = 384
CHUNKS = 2
VMEM_LIMIT = 24 * 1024 * 1024


def weigh(q, halves, top, const):
    dims = (((1,), (1,)), ((), ()))
    scores = [lax.dot_general(q, ref[0], dims, preferred_element_type=jnp.float32) for ref in halves]
    own = jnp.maximum(scores[0].max(axis=1, keepdims=True), scores[1].max(axis=1, keepdims=True))
    top, less = top(own)
    expos = [jnp.exp2((s - less) * const) for s in scores]
    total = expos[0].sum(axis=1, keepdims=True) + expos[1].sum(axis=1, keepdims=True)
    heard = sum(
        jnp.dot(e.astype(jnp.bfloat16), ref[1], preferred_element_type=jnp.float32)
        for e, ref in zip(expos, halves)
    )
    return top, total, heard


def diagonal():
    return lax.broadcasted_iota(jnp.int32, (HD, HD), 0) == lax.broadcasted_iota(jnp.int32, (HD, HD), 1)


def own_block(mask_ref, level_ref, gate_ref, q_ref, kv_ref, m_out, l_out, a_out, aux_out):
    span_at = lax.axis_index(SPAN)
    for distance in (1, 2):
        column = span_at - distance
        usable = jnp.logical_and(column >= 0, mask_ref[span_at, jnp.maximum(column, 0)] > 0)
        value = jnp.where(usable, 1.0, 0.0).astype(jnp.float32)
        aux_out[pl.ds((distance - 1) * 8, 8), :] = jnp.full((8, HD), value, jnp.float32)
    head = placed(lax.axis_index("y_lo") * lax.axis_size("z") + lax.axis_index("z"))
    mine = gate_ref[:, pl.ds(pl.multiple_of(head * HD, HD), HD)]
    chosen = lax.broadcasted_iota(jnp.int32, mine.shape, 0) == level_ref[span_at]
    gate = jnp.where(chosen, mine, 0.0).sum(axis=0, keepdims=True)
    aux_out[pl.ds(16, 8), :] = jnp.broadcast_to(gate, (8, HD))
    for t in range(q_ref.shape[0] // TILE):
        at = pl.ds(t * TILE, TILE)
        top, total, heard = weigh(q_ref[at, :], (kv_ref.at[0], kv_ref.at[1]), lambda own: (own, own), CONST)
        m_out[at, :] = jnp.broadcast_to(top, (TILE, HD))
        l_out[at, :] = jnp.broadcast_to(total, (TILE, HD))
        a_out[at, :] = heard


def served_block(q_ref, kv_ref, out_ref):
    rows = q_ref.shape[0]
    eye = diagonal()
    stats = []
    for t in range(rows // TILE):
        at = pl.ds(t * TILE, TILE)
        top, total, heard = weigh(q_ref[at, :], (kv_ref.at[0], kv_ref.at[1]), lambda own: (own, own), CONST)
        out_ref[at, :] = (heard / total).astype(jnp.bfloat16)
        level = top + jnp.log2(total) * (1.0 / CONST)
        for j in range(TILE // HD):
            stats.append(jnp.where(eye, level[j * HD : (j + 1) * HD], 0.0).sum(axis=0, keepdims=True))
    spare = 8 - len(stats)
    level = jnp.concatenate(stats + [jnp.zeros((spare, HD), jnp.float32)], axis=0)
    high = level.astype(jnp.bfloat16).astype(jnp.float32)
    middle = (level - high).astype(jnp.bfloat16).astype(jnp.float32)
    low = level - high - middle
    pieces = jnp.concatenate((high, middle, low, jnp.zeros((8, HD), jnp.float32)), axis=0)
    out_ref[pl.ds(rows, 32), :] = pieces.astype(jnp.bfloat16)


def earlier_block(aux_ref, q_ref, kv_ref, m_in, l_in, a_in, m_out, l_out, a_out):
    opened = aux_ref[0:1, :1] > 0.5
    for t in range(q_ref.shape[0] // TILE):
        at = pl.ds(t * TILE, TILE)
        before = m_in[at, :1]

        def joined(own):
            top = jnp.where(opened, jnp.maximum(own, before), before)
            return top, jnp.where(opened, top, 1e30)

        top, total, heard = weigh(q_ref[at, :], (kv_ref.at[0], kv_ref.at[1]), joined, CONST)
        shrink = jnp.exp2((before - top) * CONST)
        m_out[at, :] = jnp.broadcast_to(top, (TILE, HD))
        l_out[at, :] = jnp.broadcast_to(total + l_in[at, :1] * shrink, (TILE, HD))
        a_out[at, :] = heard + a_in[at, :] * shrink


def join(aux_ref, m_in, l_in, a_in, part_ref, out_ref):
    rows = m_in.shape[0]
    opened = aux_ref[8:9, :1] > 0.5
    gate = aux_ref[16:17, :]
    eye = diagonal()
    pieces = part_ref[pl.ds(rows, 32), :].astype(jnp.float32)
    level = pieces[0:8] + pieces[8:16] + pieces[16:24]
    for t in range(rows // HD):
        at = pl.ds(t * HD, HD)
        before = m_in[at, :]
        served = jnp.where(eye, level[t : t + 1], 0.0).sum(axis=1, keepdims=True)
        served = jnp.where(opened, served, before)
        top = jnp.maximum(before, served)
        shrink = jnp.exp2((before - top) * CONST)
        share = jnp.where(opened, jnp.exp2((served - top) * CONST), 0.0)
        total = l_in[at, :] * shrink + share
        heard = a_in[at, :] * shrink + part_ref[at, :].astype(jnp.float32) * share
        out_ref[at, :] = (heard / total * gate).astype(jnp.bfloat16)


def placed(index):
    line, depth = lax.axis_size("y_lo"), lax.axis_size("z")
    at, z = index // depth, index % depth
    return jnp.where(lax.axis_index("y_hi") > 0, line - 1 - at, at) * depth + z


def split_heads(q_hbm, k_hbm, v_hbm, out_ref, held, sems):
    wide = q_hbm.shape[2] // CHUNKS
    copies = []
    for i, source in enumerate((q_hbm, k_hbm, v_hbm)):
        for c in range(CHUNKS):
            at = pl.ds(c * wide, wide)
            copies.append(
                pltpu.make_async_copy(source.at[0, :, at], held.at[i, :, at], sems.at[i * CHUNKS + c])
            )
    for copy in copies:
        copy.start()
    each = out_ref.shape[0] // CHUNKS
    for i in range(3):
        for c in range(CHUNKS):
            copies[i * CHUNKS + c].wait()
            for h in range(c * each, (c + 1) * each):
                out_ref[placed(h), i] = held[i, :, h * HD : (h + 1) * HD]


def join_heads(in_ref, out_hbm, held, sems):
    each = in_ref.shape[0] // CHUNKS
    copies = []
    for c in range(CHUNKS):
        for h in range(c * each, (c + 1) * each):
            held[:, h * HD : (h + 1) * HD] = in_ref[placed(h)]
        at = pl.ds(c * each * HD, each * HD)
        copies.append(pltpu.make_async_copy(held.at[:, at], out_hbm.at[0, :, at], sems.at[c]))
        copies[-1].start()
    for copy in copies:
        copy.wait()


def call(kernel, out_shape, scalars, *arrays):
    vmem = pl.BlockSpec(memory_space=pltpu.VMEM)
    smem = pl.BlockSpec(memory_space=pltpu.SMEM)
    return pl.pallas_call(
        kernel,
        out_shape=out_shape,
        in_specs=[smem] * len(scalars) + [vmem] * len(arrays),
        out_specs=[vmem] * len(out_shape),
        compiler_params=pltpu.CompilerParams(vmem_limit_bytes=VMEM_LIMIT),
        cost_estimate=pl.CostEstimate(flops=1024, bytes_accessed=1024, transcendentals=0),
    )(*scalars, *arrays)


def on_device(queries, key_rows, value_rows, block_mask, noise_level, gate_table):
    local = queries.shape[1]
    heads = queries.shape[2] // HD
    spans = lax.axis_size(SPAN)
    rows = heads * local

    line = lax.axis_size("y_lo")

    def to_next(block):
        route = []
        for at, index in enumerate(np.ndindex(spans, line)):
            if index[0] + 1 < spans:
                route.append((at, (index[0] + 1) * line + line - 1 - index[1]))
        return lax.ppermute(block, SPAN + ("y_lo",), route)

    def exchange(block):
        return lax.all_to_all(block, CHIPS, split_axis=0, concat_axis=0, tiled=True)

    def moved(block, distance):
        route = [(i, i + distance) for i in range(spans) if 0 <= i + distance < spans]
        return lax.ppermute(block, SPAN, route)

    def other_core(block):
        return lax.ppermute(block, "core", [(0, 1), (1, 0)])

    def both_cores(block):
        return lax.all_gather(block, "core")

    by_head = jax.ShapeDtypeStruct((heads, 3, local, HD), queries.dtype)
    mixed = pl.pallas_call(
        split_heads,
        out_shape=by_head,
        in_specs=[pl.BlockSpec(memory_space=pltpu.HBM)] * 3,
        out_specs=pl.BlockSpec(memory_space=pltpu.VMEM),
        scratch_shapes=[
            pltpu.VMEM((3, local, heads * HD), queries.dtype),
            pltpu.SemaphoreType.DMA((3 * CHUNKS,)),
        ],
        compiler_params=pltpu.CompilerParams(vmem_limit_bytes=60 * 1024 * 1024),
    )(queries, key_rows, value_rows)
    got = exchange(mixed)
    q = got[:, 0].reshape(rows, HD)
    kv = got[:, 1:].transpose(1, 0, 2, 3).reshape(2, rows, HD)

    stat = jax.ShapeDtypeStruct((rows, HD), jnp.float32)
    aux = jax.ShapeDtypeStruct((24, HD), jnp.float32)
    part = jax.ShapeDtypeStruct((rows + 32, HD), jnp.bfloat16)
    kv1 = to_next(kv)
    later_q = moved(q, -2)
    kv0 = both_cores(kv)
    (served,) = call(served_block, [part], (), later_q, kv0)
    *state, aux = call(own_block, [stat, stat, stat, aux], (block_mask, noise_level), gate_table, q, kv0)
    part2 = moved(served, 2)
    kv1 = both_cores(kv1)
    state = call(earlier_block, [stat, stat, stat], (), aux, q, kv1, *state)
    (out,) = call(join, [jax.ShapeDtypeStruct((rows, HD), jnp.bfloat16)], (), aux, *state, part2)

    back = exchange(out.reshape(heads, local, HD))
    return pl.pallas_call(
        join_heads,
        out_shape=jax.ShapeDtypeStruct(queries.shape, queries.dtype),
        in_specs=[pl.BlockSpec(memory_space=pltpu.VMEM)],
        out_specs=pl.BlockSpec(memory_space=pltpu.HBM),
        scratch_shapes=[pltpu.VMEM((local, heads * HD), queries.dtype), pltpu.SemaphoreType.DMA((CHUNKS,))],
        compiler_params=pltpu.CompilerParams(vmem_limit_bytes=VMEM_LIMIT),
    )(back)


def solution(mesh):
    parts = Mesh(mesh.devices.reshape(4, 2, 4, 8, 2), ("x", "y_hi", "y_lo", "z", "core"))
    tokens = P(SPAN, CHIPS + ("core",), None)
    return jax.shard_map(
        on_device,
        mesh=parts,
        in_specs=(tokens, tokens, tokens, P(), P(), P()),
        out_specs=tokens,
        check_vma=False,
    )
```
